32 devices in a mesh: ctx: 8 (over y, x, core), fsdp: 4 (over z).
Axes of the slice: x: 2, y: 2, z: 4, core: 2. Of those that a mesh axis runs over, the one named last changes fastest.
Arguments:
- layer_input: bfloat16 [4, 1024, 768], P('fsdp', 'ctx'), may hold values from -6 to 6
- qkv_weight: bfloat16 [768, 2304], P('fsdp'), may hold values from -0.21875 to 0.21875
- query_bias: bfloat16 [768], P('fsdp'), may hold values from -1.5 to 1.5
- value_bias: bfloat16 [768], P('fsdp'), may hold values from -1.5 to 1.5
- out_weight: bfloat16 [768, 768], P('fsdp'), may hold values from -0.875 to 0.875
- out_bias: bfloat16 [768], P('fsdp'), may hold values from -2.5 to 2.5
- first_gain: bfloat16 [768], P('fsdp'), may hold values from 0.25 to 1.75
- first_shift: bfloat16 [768], P('fsdp'), may hold values from -1.5 to 1.5
- second_gain: bfloat16 [768], P('fsdp'), may hold values from 0.25 to 1.75
- second_shift: bfloat16 [768], P('fsdp'), may hold values from -1.5 to 1.5
- up_weight: bfloat16 [768, 3072], P('fsdp'), may hold values from -0.21875 to 0.21875
- up_bias: bfloat16 [3072], P('fsdp'), may hold values from -2.5 to 2.5
- down_weight: bfloat16 [3072, 768], P('fsdp'), may hold values from -0.109375 to 0.109375
- down_bias: bfloat16 [768], P('fsdp'), may hold values from -2.5 to 2.5
- out_grad: bfloat16 [4, 1024, 768], P('fsdp', 'ctx'), may hold values from -6 to 6
Outputs:
- layer_output: bfloat16 [4, 1024, 768], P('fsdp', 'ctx')
- input_grad: float32 [4, 1024, 768], P('fsdp', 'ctx')
- qkv_weight_grad: float32 [768, 2304], P('fsdp')
- query_bias_grad: float32 [768], P('fsdp')
- value_bias_grad: float32 [768], P('fsdp')
- out_weight_grad: float32 [768, 768], P('fsdp')
- out_bias_grad: float32 [768], P('fsdp')
- first_gain_grad: float32 [768], P('fsdp')
- first_shift_grad: float32 [768], P('fsdp')
- second_gain_grad: float32 [768], P('fsdp')
- second_shift_grad: float32 [768], P('fsdp')
- up_weight_grad: float32 [768, 3072], P('fsdp')
- up_bias_grad: float32 [3072], P('fsdp')
- down_weight_grad: float32 [3072, 768], P('fsdp')
- down_bias_grad: float32 [768], P('fsdp')
The draws below stay inside these ranges and needn't reach their ends.
All inputs are finite; a program needn't handle non-finite values.
Results may differ from the reference program's by a relative error of at most 0.018.
Values may be sent and summed in bfloat16 or wider, within the bound.
A program may use at most 128 MiB of HBM per device.

```python
import math
import jax
import jax.numpy as jnp
from jax import lax

D = 768
H = 12
HD = 64
FF = 3072
LEN = 1024
SEQS = 4


def draw_layer_input(key, part):
    key = jax.random.fold_in(key, 11)
    first = jax.random.fold_in(key, 0)
    base = jax.random.normal(first, (SEQS, LEN, D), jnp.float32)
    return jnp.clip(base, -6.0, 6.0).astype(jnp.bfloat16)


def level_of(stream_key, dims, shards, low, top_value):
    def one(dim, blocks):
        steps = jax.random.uniform(jax.random.fold_in(jax.random.fold_in(stream_key, 6), dim), (blocks,), jnp.float32, low / len(shards), top_value / len(shards))
        return jnp.repeat(jnp.exp(steps), dims[dim] // blocks).reshape((-1,) + (1,) * (len(dims) - dim - 1))

    factor_of = one(*shards[0])
    for cut in shards[1:]:
        factor_of = factor_of * one(*cut)
    return factor_of


def bell_draw(key, extent, scale, most, shards=(), dtype=jnp.bfloat16):
    entries = jax.random.normal(key, extent, jnp.float32) * scale
    if len(shards) > 0:
        entries = level_of(key, extent, shards, -0.22, 0.18) * entries
    return jnp.clip(entries, min=-most, max=most).astype(dtype)


def setup_inputs(seed: int = 0) -> dict:
    streams_of = jax.random.split(jax.random.key(seed), 16)
    layer_input = draw_layer_input(jax.random.fold_in(streams_of[15], 71), 0)
    qkv_weight = bell_draw(streams_of[1], (D, 3 * D), D ** -0.5, 0.21875, ((0, 4),))
    query_bias = bell_draw(streams_of[2], (D,), 0.3, 1.5, ((0, 4),))
    value_bias = bell_draw(streams_of[3], (D,), 0.3, 1.5, ((0, 4),))
    out_weight = bell_draw(streams_of[4], (D, D), (D // 16) ** -0.5, 0.875, ((0, 4),))
    out_bias = bell_draw(streams_of[5], (D,), 0.5, 2.5, ((0, 4),))
    first_gain = jnp.clip(1.0 + 0.15 * jax.random.normal(streams_of[6], (D,), jnp.float32), 0.25, 1.75).astype(jnp.bfloat16)
    first_shift = bell_draw(streams_of[7], (D,), 0.3, 1.5, ((0, 4),))
    second_gain = jnp.clip(1.0 + 0.15 * jax.random.normal(streams_of[8], (D,), jnp.float32), 0.25, 1.75).astype(jnp.bfloat16)
    second_shift = bell_draw(streams_of[9], (D,), 0.3, 1.5, ((0, 4),))
    up_weight = bell_draw(streams_of[10], (D, FF), D ** -0.5, 0.21875, ((0, 4),))
    up_bias = bell_draw(streams_of[11], (FF,), 0.5, 2.5, ((0, 4),))
    down_weight = bell_draw(streams_of[12], (FF, D), FF ** -0.5, 0.109375, ((0, 4),))
    down_bias = bell_draw(streams_of[13], (D,), 0.5, 2.5, ((0, 4),))
    out_grad = bell_draw(streams_of[14], (SEQS, LEN, D), 1.0, 6.0, ((0, 4), (1, 8)))
    return {"layer_input": layer_input, "qkv_weight": qkv_weight, "query_bias": query_bias, "value_bias": value_bias, "out_weight": out_weight, "out_bias": out_bias, "first_gain": first_gain, "first_shift": first_shift, "second_gain": second_gain, "second_shift": second_shift, "up_weight": up_weight, "up_bias": up_bias, "down_weight": down_weight, "down_bias": down_bias, "out_grad": out_grad}


EPS = 1e-05
NEG = -1e+30
GELU_C = 0.7978845608028654
GELU_A = 0.044715

def gelu_pair(values):
    inner = GELU_C * (values + GELU_A * values * values * values)
    tanh_val = jnp.tanh(inner)
    result = 0.5 * values * (1.0 + tanh_val)
    slope = 0.5 * (1.0 + tanh_val) + 0.5 * values * (1.0 - tanh_val * tanh_val) * GELU_C * (1.0 + 3.0 * GELU_A * values * values)
    return (result, slope)

def norm_rows(values, gain, shift):
    mean = lax.optimization_barrier(jnp.mean(values, axis=-1, keepdims=True))
    centred = values - mean
    inv_std = lax.rsqrt(lax.optimization_barrier(jnp.mean(centred * centred, axis=-1, keepdims=True)) + EPS)
    normed = centred * inv_std
    return (normed * gain.astype(jnp.float32) + shift.astype(jnp.float32), normed, inv_std)

def norm_back(grad_out, normed, inv_std, gain):
    scaled = grad_out * gain.astype(jnp.float32)
    return inv_std * (scaled - lax.optimization_barrier(jnp.mean(scaled, axis=-1, keepdims=True)) - normed * lax.optimization_barrier(jnp.mean(scaled * normed, axis=-1, keepdims=True)))

def matmul(left, right):
    return jnp.dot(left, right, preferred_element_type=jnp.float32)

def causal_table(size):
    return jnp.arange(size)[:, None] >= jnp.arange(size)[None, :]

def head_forward(items):
    query, keys, values = items
    scale = 1.0 / math.sqrt(query.shape[-1])
    scores = matmul(query, keys.T) * scale
    causal = causal_table(query.shape[0])
    masked = jnp.where(causal, scores, NEG)
    top = lax.optimization_barrier(jnp.max(masked, axis=1))
    total = lax.optimization_barrier(jnp.sum(jnp.where(causal, jnp.exp(masked - top[:, None]), 0.0), axis=1))
    logsum = top + jnp.log(total)
    weights = jnp.where(causal, jnp.exp(scores - logsum[:, None]), 0.0)
    mixed = jnp.dot(weights, values.astype(jnp.float32), precision=lax.Precision.HIGHEST, preferred_element_type=jnp.float32)
    return (mixed.astype(jnp.bfloat16), logsum)

def head_backward(items):
    query, keys, values, grad_head, logsum, delta = items
    scale = 1.0 / math.sqrt(query.shape[-1])
    scores = matmul(query, keys.T) * scale
    causal = causal_table(query.shape[0])
    probs = jnp.where(causal, jnp.exp(scores - logsum[:, None]), 0.0)
    grad_values = matmul(probs.astype(jnp.bfloat16).T, grad_head)
    grad_probs = matmul(grad_head, values.T)
    grad_scores = (probs * (grad_probs - delta[:, None])).astype(jnp.bfloat16)
    grad_query = matmul(grad_scores, keys) * scale
    grad_keys = matmul(grad_scores.T, query) * scale
    return (grad_query, grad_keys, grad_values)

def split_heads(rows):
    length = rows.shape[0]
    return rows.reshape(length, H, HD).transpose(1, 0, 2)

def join_heads(heads):
    length = heads.shape[1]
    return heads.transpose(1, 0, 2).reshape(length, H * HD)

def sequence_pass(inputs_bf, upstream, params):
    qkv_weight, query_bias, value_bias, out_weight, out_bias, first_gain, first_shift, second_gain, second_shift, up_weight, up_bias, down_weight, down_bias = params
    width = inputs_bf.shape[1]
    inputs = inputs_bf.astype(jnp.float32)
    normed_one, unit_one, inv_one = norm_rows(inputs, first_gain, first_shift)
    mixed_in = normed_one.astype(jnp.bfloat16)
    projected = matmul(mixed_in, qkv_weight)
    queries = (projected[:, :width] + query_bias.astype(jnp.float32)).astype(jnp.bfloat16)
    keys = projected[:, width:2 * width].astype(jnp.bfloat16)
    values = (projected[:, 2 * width:] + value_bias.astype(jnp.float32)).astype(jnp.bfloat16)
    query_heads = split_heads(queries)
    key_heads = split_heads(keys)
    value_heads = split_heads(values)
    out_heads, logsum = lax.map(head_forward, (query_heads, key_heads, value_heads))
    attended = join_heads(out_heads)
    hidden = inputs + matmul(attended, out_weight) + out_bias.astype(jnp.float32)
    normed_two, unit_two, inv_two = norm_rows(hidden, second_gain, second_shift)
    ffn_in = normed_two.astype(jnp.bfloat16)
    lifted = matmul(ffn_in, up_weight) + up_bias.astype(jnp.float32)
    gelu_val, gelu_slope = gelu_pair(lifted)
    active = gelu_val.astype(jnp.bfloat16)
    result = hidden + matmul(active, down_weight) + down_bias.astype(jnp.float32)
    layer_output = result.astype(jnp.bfloat16)
    upstream_f = upstream.astype(jnp.float32)
    grad_down_bias = lax.optimization_barrier(jnp.sum(upstream_f, axis=0))
    grad_down = matmul(active.T, upstream)
    grad_active = matmul(upstream, down_weight.T)
    grad_lifted = grad_active * gelu_slope
    lifted_b = grad_lifted.astype(jnp.bfloat16)
    grad_up_bias = lax.optimization_barrier(jnp.sum(grad_lifted, axis=0))
    grad_up = matmul(ffn_in.T, lifted_b)
    grad_normed_two = matmul(lifted_b, up_weight.T)
    grad_second_gain = lax.optimization_barrier(jnp.sum(grad_normed_two * unit_two, axis=0))
    grad_second_shift = lax.optimization_barrier(jnp.sum(grad_normed_two, axis=0))
    grad_hidden = upstream_f + norm_back(grad_normed_two, unit_two, inv_two, second_gain)
    hidden_b = grad_hidden.astype(jnp.bfloat16)
    grad_out_bias = lax.optimization_barrier(jnp.sum(grad_hidden, axis=0))
    grad_out = matmul(attended.T, hidden_b)
    grad_attended = matmul(hidden_b, out_weight.T).astype(jnp.bfloat16)
    grad_heads = split_heads(grad_attended)
    delta = lax.optimization_barrier(jnp.sum(grad_heads.astype(jnp.float32) * out_heads.astype(jnp.float32), axis=-1))
    grad_q, grad_k, grad_v = lax.map(head_backward, (query_heads, key_heads, value_heads, grad_heads, logsum, delta))
    grad_queries = join_heads(grad_q)
    grad_values = join_heads(grad_v)
    grad_proj = jnp.concatenate([grad_queries, join_heads(grad_k), grad_values], axis=1)
    proj_b = grad_proj.astype(jnp.bfloat16)
    grad_qkv = matmul(mixed_in.T, proj_b)
    grad_query_bias = lax.optimization_barrier(jnp.sum(grad_queries, axis=0))
    grad_value_bias = lax.optimization_barrier(jnp.sum(grad_values, axis=0))
    grad_normed_one = matmul(proj_b, qkv_weight.T)
    grad_first_gain = lax.optimization_barrier(jnp.sum(grad_normed_one * unit_one, axis=0))
    grad_first_shift = lax.optimization_barrier(jnp.sum(grad_normed_one, axis=0))
    input_grad = grad_hidden + norm_back(grad_normed_one, unit_one, inv_one, first_gain)
    grads = (grad_qkv, grad_query_bias, grad_value_bias, grad_out, grad_out_bias, grad_first_gain, grad_first_shift, grad_second_gain, grad_second_shift, grad_up, grad_up_bias, grad_down, grad_down_bias)
    return (layer_output, input_grad, grads)

def reference(layer_input, qkv_weight, query_bias, value_bias, out_weight, out_bias, first_gain, first_shift, second_gain, second_shift, up_weight, up_bias, down_weight, down_bias, out_grad):
    params = (qkv_weight, query_bias, value_bias, out_weight, out_bias, first_gain, first_shift, second_gain, second_shift, up_weight, up_bias, down_weight, down_bias)

    def visit(carry, items):
        inputs_bf, upstream = items
        layer_output, input_grad, grads = sequence_pass(inputs_bf, upstream, params)
        return (tuple((a + b for a, b in zip(carry, grads))), (layer_output, input_grad))
    start = tuple((jnp.zeros(p.shape, jnp.float32) for p in params))
    grads, (outputs, input_grads) = lax.scan(visit, start, (layer_input, out_grad))
    return (outputs, input_grads, grads[0], grads[1], grads[2], grads[3], grads[4], grads[5], grads[6], grads[7], grads[8], grads[9], grads[10], grads[11], grads[12])
```

```python
import functools
import math

import jax
import jax.numpy as jnp
from jax import lax
from jax.experimental import pallas as pl
from jax.experimental.pallas import tpu as pltpu
from jax.sharding import PartitionSpec as P

HD = 64
EPS = 1e-05
NEG = -1e30
GELU_C = 0.7978845608028654
GELU_A = 0.044715
MESH = pl.DeviceIdType.MESH
BF = jnp.bfloat16
F32 = jnp.float32


def gelu_pair(values):
    inner = GELU_C * (values + GELU_A * values * values * values)
    tanh_val = jnp.tanh(inner)
    result = 0.5 * values * (1.0 + tanh_val)
    slope = 0.5 * (1.0 + tanh_val) + 0.5 * values * (1.0 - tanh_val * tanh_val) * GELU_C * (
        1.0 + 3.0 * GELU_A * values * values
    )
    return (result, slope)


def norm_rows(values, gain, shift):
    mean = jnp.mean(values, axis=-1, keepdims=True)
    centred = values - mean
    inv_std = lax.rsqrt(jnp.mean(centred * centred, axis=-1, keepdims=True) + EPS)
    normed = centred * inv_std
    return (normed * gain + shift, normed, inv_std)


def norm_back(grad_out, normed, inv_std, gain):
    scaled = grad_out * gain
    return inv_std * (
        scaled
        - jnp.mean(scaled, axis=-1, keepdims=True)
        - normed * jnp.mean(scaled * normed, axis=-1, keepdims=True)
    )


def matmul(left, right):
    return jnp.dot(left, right, preferred_element_type=F32)


def inner_rows(left, right):
    return lax.dot_general(left, right, (((0,), (0,)), ((), ())), preferred_element_type=F32)


def outer_cols(left, right):
    return lax.dot_general(left, right, (((1,), (1,)), ((), ())), preferred_element_type=F32)


def greet(devices):
    barrier = pltpu.get_barrier_semaphore()
    for device in devices:
        pl.semaphore_signal(barrier, inc=1, device_id=device, device_id_type=MESH)
    pl.semaphore_wait(barrier, len(devices))


def push(src, dst, send_sem, recv_sem, device):
    return pltpu.make_async_remote_copy(
        src_ref=src, dst_ref=dst, send_sem=send_sem, recv_sem=recv_sem,
        device_id=device, device_id_type=MESH,
    )


def gather_kernel(n, m, a_count, z_count, *refs):
    ins = refs[: a_count + z_count]
    outs = refs[a_count + z_count : 2 * (a_count + z_count)]
    a_send, a_recv, a_fwd, z_send, z_recv, local = refs[2 * (a_count + z_count) :]
    me, zed = lax.axis_index("ctx"), lax.axis_index("fsdp")
    core, chip = lax.rem(me, 2), lax.div(me, 2)
    chips = n // 2
    sib = me + 1 - 2 * core
    peers = [2 * lax.rem(chip + k, chips) + core for k in range(1, chips)]
    sources = [2 * lax.rem(chip + chips - k, chips) + core for k in range(1, chips)]
    zeds = [lax.rem(zed + k, m) for k in range(1, m)]
    devices = []
    if a_count:
        devices += [(sib, zed)] + [(p, zed) for p in peers]
    if z_count:
        devices += [(me, z) for z in zeds]
    greet(devices)
    sends = []
    locals_ = []
    for a in range(a_count):
        for k, p in enumerate(peers):
            sends.append(push(ins[a], outs[a].at[me], a_send.at[a, k], a_recv.at[a, me], (p, zed)))
            sends[-1].start()
        sends.append(
            push(ins[a], outs[a].at[me], a_send.at[a, chips - 1], a_recv.at[a, me], (sib, zed))
        )
        sends[-1].start()
    for i in range(z_count):
        b = a_count + i
        for k, z in enumerate(zeds):
            sends.append(push(ins[b], outs[b].at[zed], z_send.at[i, k], z_recv.at[i, zed], (me, z)))
            sends[-1].start()
    for b in range(a_count + z_count):
        slot = me if b < a_count else zed
        locals_.append(pltpu.make_async_copy(ins[b], outs[b].at[slot], local.at[b]))
        locals_[-1].start()
    for a in range(a_count):
        for k, s in enumerate(sources):
            push(ins[a], outs[a].at[s], a_fwd.at[a, k], a_recv.at[a, s], (sib, zed)).wait_recv()
            sends.append(
                push(outs[a].at[s], outs[a].at[s], a_fwd.at[a, k], a_recv.at[a, s], (sib, zed))
            )
            sends[-1].start()
    for a in range(a_count):
        for s in [sib] + [s + 1 - 2 * core for s in sources]:
            push(ins[a], outs[a].at[s], a_send.at[a, 0], a_recv.at[a, s], (sib, zed)).wait_recv()
    for i in range(z_count):
        b = a_count + i
        for z in zeds:
            push(ins[b], outs[b].at[z], z_send.at[i, 0], z_recv.at[i, z], (me, z)).wait_recv()
    for copy in locals_:
        copy.wait()
    for copy in sends:
        copy.wait_send()


def gather(n, m, over_ctx, over_fsdp, ident):
    arrays = tuple(over_ctx) + tuple(over_fsdp)
    a, z = len(over_ctx), len(over_fsdp)
    out_shape = [jax.ShapeDtypeStruct((n,) + v.shape, v.dtype) for v in over_ctx]
    out_shape += [jax.ShapeDtypeStruct((m,) + v.shape, v.dtype) for v in over_fsdp]
    dma = pltpu.SemaphoreType.DMA
    return pl.pallas_call(
        functools.partial(gather_kernel, n, m, a, z),
        out_shape=out_shape,
        in_specs=[pl.BlockSpec(memory_space=pl.ANY)] * (a + z),
        out_specs=[pl.BlockSpec(memory_space=pl.ANY)] * (a + z),
        scratch_shapes=[
            dma((max(a, 1), n // 2)),
            dma((max(a, 1), n)),
            dma((max(a, 1), n // 2)),
            dma((max(z, 1), m)),
            dma((max(z, 1), m)),
            dma((a + z,)),
        ],
        compiler_params=pltpu.CompilerParams(collective_id=ident, has_side_effects=True),
    )(*arrays)


def scatter_kernel(n, x_ref, o_ref, one, pair, two, s1, r1, s2, r2):
    me, zed = lax.axis_index("ctx"), lax.axis_index("fsdp")
    core, chip = lax.rem(me, 2), lax.div(me, 2)
    chips = n // 2
    sib = me + 1 - 2 * core
    order = [lax.rem(chip + k, chips) for k in range(1, chips)] + [chip]
    greet([(sib, zed)] + [(2 * j + core, zed) for j in order[:-1]])
    first = []
    for k, j in enumerate(order):
        first.append(push(x_ref.at[2 * j + 1 - core], one.at[k], s1.at[k], r1.at[k], (sib, zed)))
        first[-1].start()
    second = []
    for k, j in enumerate(order):
        first[k].wait_recv()
        total = x_ref[2 * j + core].astype(F32) + one[k].astype(F32)
        if k < chips - 1:
            pair[k] = total.astype(BF)
            second.append(
                push(pair.at[k], two.at[k], s2.at[k], r2.at[k], (2 * j + core, zed))
            )
            second[-1].start()
        else:
            o_ref[...] = total
    for k in range(chips - 1):
        second[k].wait_recv()
        o_ref[...] += two[k].astype(F32)
    for copy in first + second:
        copy.wait_send()


def scatter(n, x, ident):
    _, rows, cols = x.shape
    chips = n // 2
    dma = pltpu.SemaphoreType.DMA
    return pl.pallas_call(
        functools.partial(scatter_kernel, n),
        out_shape=jax.ShapeDtypeStruct((rows, cols), F32),
        in_specs=[pl.BlockSpec(memory_space=pltpu.VMEM)],
        out_specs=pl.BlockSpec(memory_space=pltpu.VMEM),
        scratch_shapes=[
            pltpu.VMEM((chips, rows, cols), BF),
            pltpu.VMEM((chips - 1, rows, cols), BF),
            pltpu.VMEM((chips - 1, rows, cols), BF),
            dma((chips,)),
            dma((chips,)),
            dma((chips - 1,)),
            dma((chips - 1,)),
        ],
        compiler_params=pltpu.CompilerParams(
            collective_id=ident, has_side_effects=True, vmem_limit_bytes=48 << 20
        ),
    )(x)


def swap_kernel(n, x_ref, o_ref, send, recv, local):
    me, zed = lax.axis_index("ctx"), lax.axis_index("fsdp")
    others = [lax.rem(me + k, n) for k in range(1, n)]
    greet([(j, zed) for j in others])
    sends = []
    for k, j in enumerate(others):
        sends.append(push(x_ref.at[j], o_ref.at[me], send.at[k], recv.at[me], (j, zed)))
        sends[-1].start()
    own = pltpu.make_async_copy(x_ref.at[me], o_ref.at[me], local)
    own.start()
    own.wait()
    for k, j in enumerate(others):
        push(x_ref.at[j], o_ref.at[j], send.at[k], recv.at[j], (j, zed)).wait_recv()
    for copy in sends:
        copy.wait_send()


def swap(n, x, ident):
    dma = pltpu.SemaphoreType.DMA
    return pl.pallas_call(
        functools.partial(swap_kernel, n),
        out_shape=jax.ShapeDtypeStruct(x.shape, x.dtype),
        in_specs=[pl.BlockSpec(memory_space=pltpu.VMEM)],
        out_specs=pl.BlockSpec(memory_space=pltpu.VMEM),
        scratch_shapes=[dma((n,)), dma((n,)), dma],
        compiler_params=pltpu.CompilerParams(collective_id=ident, has_side_effects=True),
    )(x)


def shards(
    n,
    m,
    layer_input,
    qkv_weight,
    query_bias,
    value_bias,
    out_weight,
    out_bias,
    first_gain,
    first_shift,
    second_gain,
    second_shift,
    up_weight,
    up_bias,
    down_weight,
    down_bias,
    out_grad,
):
    seqs, block, width = layer_input.shape
    rows = seqs * block
    length = n * block
    heads = width // HD
    scale = 1.0 / math.sqrt(HD)
    me, zed = lax.axis_index("ctx"), lax.axis_index("fsdp")
    hp = -(-heads // n)
    while heads % hp:
        hp += 1
    active_n = heads // hp
    hw = hp * HD
    valid = me < active_n
    head_at = jnp.minimum(me, active_n - 1)
    share = width // m
    hidden_share = up_bias.shape[0]
    fpart = hidden_share // n
    ff = hidden_share * m
    fown = m * fpart

    x_local = layer_input.reshape(rows, width)
    g_local = out_grad.reshape(rows, width)
    qkv_own = lax.dynamic_index_in_dim(
        qkv_weight.reshape(share, 3, active_n, hw), head_at, 2, keepdims=False
    ).reshape(share, 3 * hw)
    up_own = lax.dynamic_index_in_dim(
        up_weight.reshape(share, m, n, fpart), me, 2, keepdims=False
    ).reshape(share, fown)
    down_own = lax.dynamic_index_in_dim(
        down_weight.reshape(n, fpart, width), me, 0, keepdims=False
    )
    out_own = lax.dynamic_index_in_dim(
        out_weight.reshape(n, share // n, width), me, 0, keepdims=False
    )
    vectors = jnp.concatenate(
        [query_bias, value_bias, out_bias, first_gain, first_shift, second_gain, second_shift,
         down_bias, up_bias]
    ).astype(F32)
    span = vectors.shape[0]
    padded = -(-span // 1024) * 1024
    vectors = jnp.pad(vectors, (0, padded - span)).reshape(padded // 128, 128)

    x_all, qkv_all, vec_all = gather(n, m, [x_local], [qkv_own, vectors], 0)
    up_mat = lax.all_gather(up_own, "fsdp", axis=0, tiled=True)
    down_mat = lax.all_gather(down_own, "fsdp", axis=0, tiled=True)
    out_mat = lax.all_gather(out_own, ("fsdp", "ctx"), axis=0, tiled=True)
    g_all = lax.all_gather(g_local, "ctx", axis=0, tiled=True)

    qkv_mat = jnp.where(valid, qkv_all.reshape(width, 3 * hw), jnp.zeros((), BF))
    vec_all = vec_all.reshape(m, padded)
    pieces = [vec_all[:, i * share : (i + 1) * share].reshape(width) for i in range(8)]
    q_bias, v_bias, out_shift, gain_one, shift_one, gain_two, shift_two, down_shift = pieces
    up_shift = lax.dynamic_index_in_dim(
        vec_all[:, 8 * share : span].reshape(m, n, fpart), me, 1, keepdims=False
    ).reshape(fown)
    q_own = lax.dynamic_index_in_dim(q_bias.reshape(active_n, hw), head_at, 0, keepdims=False)
    v_own = lax.dynamic_index_in_dim(v_bias.reshape(active_n, hw), head_at, 0, keepdims=False)

    def to_seq(v):
        return (
            v.reshape(n, seqs, block, hp, HD)
            .transpose(1, 3, 0, 2, 4)
            .reshape(seqs, hp, length, HD)
        )

    def from_seq(v):
        return (
            v.reshape(seqs, hp, n, block, HD)
            .transpose(2, 0, 3, 1, 4)
            .reshape(n * rows, hw)
        )

    x_rows = x_all.reshape(n * rows, width).astype(F32)
    normed_all, _, _ = norm_rows(x_rows, gain_one, shift_one)
    mixed_in = normed_all.astype(BF)
    projected = matmul(mixed_in, qkv_mat)
    queries = to_seq((projected[:, :hw] + q_own).astype(BF))
    keys = to_seq(projected[:, hw : 2 * hw].astype(BF))
    values = to_seq((projected[:, 2 * hw :] + v_own).astype(BF))

    at = jnp.arange(length, dtype=jnp.int32)
    causal = (at[None, :] <= at[:, None])[None, None]
    scores = jnp.einsum("shqd,shkd->shqk", queries, keys, preferred_element_type=F32) * scale
    masked = jnp.where(causal, scores, NEG)
    top = jnp.max(masked, axis=-1)
    total = jnp.sum(jnp.exp(masked - top[..., None]), axis=-1)
    logsum = top + jnp.log(total)
    probs = jnp.where(causal, jnp.exp(scores - logsum[..., None]), 0.0)
    probs_b = probs.astype(BF)
    mixed = jnp.einsum("shqk,shkd->shqd", probs_b, values, preferred_element_type=F32).astype(BF)

    got = swap(n, from_seq(mixed).reshape(n, rows, hw), 1)
    attended = got[:active_n].transpose(1, 0, 2).reshape(rows, width)
    inputs = x_local.astype(F32)
    _, unit_one, inv_one = norm_rows(inputs, gain_one, shift_one)
    hidden = inputs + matmul(attended, out_mat) + out_shift
    normed_two, unit_two, inv_two = norm_rows(hidden, gain_two, shift_two)
    (ffn_in,) = gather(n, m, [normed_two.astype(BF)], [], 2)
    ffn_in = ffn_in.reshape(n * rows, width)
    lifted = matmul(ffn_in, up_mat) + up_shift
    gelu_val, gelu_slope = gelu_pair(lifted)
    active = gelu_val.astype(BF)

    grad_lifted = outer_cols(g_all, down_mat) * gelu_slope
    lifted_b = grad_lifted.astype(BF)
    part_two = outer_cols(lifted_b, up_mat).astype(BF).reshape(n, rows, width)
    grad_normed_two = scatter(n, part_two, 3)

    down_part = matmul(active, down_mat).astype(BF)
    result = hidden + down_shift + lax.psum_scatter(
        down_part, "ctx", scatter_dimension=0, tiled=True
    ).astype(F32)
    layer_output = result.astype(BF).reshape(seqs, block, width)
    grad_up_shift = jnp.sum(grad_lifted, axis=0)
    grad_down = inner_rows(active, g_all).astype(BF)
    grad_up = inner_rows(ffn_in, lifted_b).astype(BF)
    grad_down = lax.psum_scatter(grad_down, "fsdp", scatter_dimension=0, tiled=True)
    grad_up = lax.psum_scatter(grad_up, "fsdp", scatter_dimension=0, tiled=True)
    grad_down = lax.all_gather(grad_down, "ctx", axis=0, tiled=True).astype(F32)
    grad_up = (
        lax.all_gather(grad_up, "ctx", axis=0)
        .reshape(n, share, m, fpart)
        .transpose(1, 2, 0, 3)
        .reshape(share, ff)
        .astype(F32)
    )

    upstream_f = g_local.astype(F32)
    grad_gain_two = jnp.sum(grad_normed_two * unit_two, axis=0)
    grad_shift_two = jnp.sum(grad_normed_two, axis=0)
    grad_hidden = upstream_f + norm_back(grad_normed_two, unit_two, inv_two, gain_two)
    hidden_b = grad_hidden.astype(BF)
    grad_out_shift = jnp.sum(grad_hidden, axis=0)
    grad_attended = outer_cols(hidden_b, out_mat).astype(BF)
    blocks = grad_attended.reshape(rows, active_n, hw).transpose(1, 0, 2)
    blocks = jnp.pad(blocks, ((0, n - active_n), (0, 0), (0, 0)))
    grad_heads = to_seq(swap(n, blocks, 4).reshape(n * rows, hw))

    grad_out = inner_rows(attended, hidden_b).astype(BF)
    grad_out = lax.psum_scatter(grad_out, ("fsdp", "ctx"), scatter_dimension=0, tiled=True)
    grad_out = lax.all_gather(grad_out, "ctx", axis=0, tiled=True).astype(F32)

    delta = jnp.sum(grad_heads.astype(F32) * mixed.astype(F32), axis=-1)
    grad_probs = jnp.einsum("shqd,shkd->shqk", grad_heads, values, preferred_element_type=F32)
    grad_scores = (probs * (grad_probs - delta[..., None])).astype(BF)
    grad_values = jnp.einsum("shqk,shqd->shkd", probs_b, grad_heads, preferred_element_type=F32)
    grad_queries = (
        jnp.einsum("shqk,shkd->shqd", grad_scores, keys, preferred_element_type=F32) * scale
    )
    grad_keys = (
        jnp.einsum("shqk,shqd->shkd", grad_scores, queries, preferred_element_type=F32) * scale
    )
    grad_query_shift = jnp.sum(grad_queries, axis=(0, 2)).reshape(hw)
    grad_value_shift = jnp.sum(grad_values, axis=(0, 2)).reshape(hw)
    proj_b = jnp.concatenate(
        [from_seq(g.astype(BF)) for g in (grad_queries, grad_keys, grad_values)], axis=1
    )
    part_one = outer_cols(proj_b, qkv_mat).astype(BF).reshape(n, rows, width)
    grad_qkv = inner_rows(mixed_in, proj_b).astype(BF)
    grad_qkv = lax.psum_scatter(grad_qkv, "fsdp", scatter_dimension=0, tiled=True)
    grad_normed_one = scatter(n, part_one, 5)
    grad_qkv = (
        lax.all_gather(grad_qkv, "ctx", axis=0)[:active_n]
        .reshape(active_n, share, 3, hw)
        .transpose(1, 2, 0, 3)
        .reshape(share, 3 * width)
        .astype(F32)
    )
    grad_gain_one = jnp.sum(grad_normed_one * unit_one, axis=0)
    grad_shift_one = jnp.sum(grad_normed_one, axis=0)
    input_grad = (grad_hidden + norm_back(grad_normed_one, unit_one, inv_one, gain_one)).reshape(
        seqs, block, width
    )

    def place_heads(v):
        spot = (jnp.arange(active_n, dtype=jnp.int32) == me)[:, None]
        return jnp.where(spot, v[None, :], 0.0).reshape(width)

    spot = (jnp.arange(n, dtype=jnp.int32) == me)[None, :, None]
    up_placed = jnp.where(spot, grad_up_shift.reshape(m, 1, fpart), 0.0).reshape(ff)
    small = jnp.concatenate(
        [
            place_heads(grad_query_shift), place_heads(grad_value_shift), grad_out_shift,
            grad_gain_one, grad_shift_one, grad_gain_two, grad_shift_two,
            jnp.sum(upstream_f, axis=0), up_placed,
        ]
    )
    small = lax.psum(small, ("fsdp", "ctx"))
    mine = lax.dynamic_index_in_dim(
        small[: 8 * width].reshape(8, m, share), zed, 1, keepdims=False
    )
    up_mine = lax.dynamic_index_in_dim(
        small[8 * width :].reshape(m, hidden_share), zed, 0, keepdims=False
    )
    return (
        layer_output,
        input_grad,
        grad_qkv,
        mine[0],
        mine[1],
        grad_out,
        mine[2],
        mine[3],
        mine[4],
        mine[5],
        mine[6],
        grad_up,
        up_mine,
        grad_down,
        mine[7],
    )


def solution(mesh):
    vec, mat, act = P("fsdp"), P("fsdp", None), P("fsdp", "ctx", None)
    n, m = mesh.shape["ctx"], mesh.shape["fsdp"]
    return jax.shard_map(
        functools.partial(shards, n, m),
        mesh=mesh,
        in_specs=(act, mat, vec, vec, mat, vec, vec, vec, vec, vec, mat, vec, mat, vec, act),
        out_specs=(act, act, mat, vec, vec, mat, vec, vec, vec, vec, vec, mat, vec, mat, vec),
        check_vma=False,
    )
```

```python
import functools
import math

import jax
import jax.numpy as jnp
from jax import lax
from jax.experimental import pallas as pl
from jax.experimental.pallas import tpu as pltpu
from jax.sharding import PartitionSpec as P

HD = 64
EPS = 1e-05
NEG = -1e30
GELU_C = 0.7978845608028654
GELU_A = 0.044715
MESH = pl.DeviceIdType.MESH
BF = jnp.bfloat16
F32 = jnp.float32


def gelu_pair(values):
    inner = GELU_C * (values + GELU_A * values * values * values)
    tanh_val = jnp.tanh(inner)
    result = 0.5 * values * (1.0 + tanh_val)
    slope = 0.5 * (1.0 + tanh_val) + 0.5 * values * (1.0 - tanh_val * tanh_val) * GELU_C * (
        1.0 + 3.0 * GELU_A * values * values
    )
    return (result, slope)


def norm_rows(values, gain, shift):
    mean = jnp.mean(values, axis=-1, keepdims=True)
    centred = values - mean
    inv_std = lax.rsqrt(jnp.mean(centred * centred, axis=-1, keepdims=True) + EPS)
    normed = centred * inv_std
    return (normed * gain + shift, normed, inv_std)


def norm_back(grad_out, normed, inv_std, gain):
    scaled = grad_out * gain
    return inv_std * (
        scaled
        - jnp.mean(scaled, axis=-1, keepdims=True)
        - normed * jnp.mean(scaled * normed, axis=-1, keepdims=True)
    )


def matmul(left, right):
    return jnp.dot(left, right, preferred_element_type=F32)


def inner_rows(left, right):
    return lax.dot_general(left, right, (((0,), (0,)), ((), ())), preferred_element_type=F32)


def outer_cols(left, right):
    return lax.dot_general(left, right, (((1,), (1,)), ((), ())), preferred_element_type=F32)


def greet(devices):
    barrier = pltpu.get_barrier_semaphore()
    for device in devices:
        pl.semaphore_signal(barrier, inc=1, device_id=device, device_id_type=MESH)
    pl.semaphore_wait(barrier, len(devices))


def push(src, dst, send_sem, recv_sem, device):
    return pltpu.make_async_remote_copy(
        src_ref=src, dst_ref=dst, send_sem=send_sem, recv_sem=recv_sem,
        device_id=device, device_id_type=MESH,
    )


def gather_kernel(n, m, a_count, z_count, *refs):
    ins = refs[: a_count + z_count]
    outs = refs[a_count + z_count : 2 * (a_count + z_count)]
    a_send, a_recv, a_fwd, z_send, z_recv, local = refs[2 * (a_count + z_count) :]
    me, zed = lax.axis_index("ctx"), lax.axis_index("fsdp")
    core, chip = lax.rem(me, 2), lax.div(me, 2)
    chips = n // 2
    sib = me + 1 - 2 * core
    peers = [2 * lax.rem(chip + k, chips) + core for k in range(1, chips)]
    sources = [2 * lax.rem(chip + chips - k, chips) + core for k in range(1, chips)]
    zeds = [lax.rem(zed + k, m) for k in range(1, m)]
    devices = []
    if a_count:
        devices += [(sib, zed)] + [(p, zed) for p in peers]
    if z_count:
        devices += [(me, z) for z in zeds]
    greet(devices)
    sends = []
    locals_ = []
    for a in range(a_count):
        for k, p in enumerate(peers):
            sends.append(push(ins[a], outs[a].at[me], a_send.at[a, k], a_recv.at[a, me], (p, zed)))
            sends[-1].start()
        sends.append(
            push(ins[a], outs[a].at[me], a_send.at[a, chips - 1], a_recv.at[a, me], (sib, zed))
        )
        sends[-1].start()
    for i in range(z_count):
        b = a_count + i
        for k, z in enumerate(zeds):
            sends.append(push(ins[b], outs[b].at[zed], z_send.at[i, k], z_recv.at[i, zed], (me, z)))
            sends[-1].start()
    for b in range(a_count + z_count):
        slot = me if b < a_count else zed
        locals_.append(pltpu.make_async_copy(ins[b], outs[b].at[slot], local.at[b]))
        locals_[-1].start()
    for a in range(a_count):
        for k, s in enumerate(sources):
            push(ins[a], outs[a].at[s], a_fwd.at[a, k], a_recv.at[a, s], (sib, zed)).wait_recv()
            sends.append(
                push(outs[a].at[s], outs[a].at[s], a_fwd.at[a, k], a_recv.at[a, s], (sib, zed))
            )
            sends[-1].start()
    for a in range(a_count):
        for s in [sib] + [s + 1 - 2 * core for s in sources]:
            push(ins[a], outs[a].at[s], a_send.at[a, 0], a_recv.at[a, s], (sib, zed)).wait_recv()
    for i in range(z_count):
        b = a_count + i
        for z in zeds:
            push(ins[b], outs[b].at[z], z_send.at[i, 0], z_recv.at[i, z], (me, z)).wait_recv()
    for copy in locals_:
        copy.wait()
    for copy in sends:
        copy.wait_send()


def gather(n, m, over_ctx, over_fsdp, ident):
    arrays = tuple(over_ctx) + tuple(over_fsdp)
    a, z = len(over_ctx), len(over_fsdp)
    out_shape = [jax.ShapeDtypeStruct((n,) + v.shape, v.dtype) for v in over_ctx]
    out_shape += [jax.ShapeDtypeStruct((m,) + v.shape, v.dtype) for v in over_fsdp]
    dma = pltpu.SemaphoreType.DMA
    return pl.pallas_call(
        functools.partial(gather_kernel, n, m, a, z),
        out_shape=out_shape,
        in_specs=[pl.BlockSpec(memory_space=pl.ANY)] * (a + z),
        out_specs=[pl.BlockSpec(memory_space=pl.ANY)] * (a + z),
        scratch_shapes=[
            dma((max(a, 1), n // 2)),
            dma((max(a, 1), n)),
            dma((max(a, 1), n // 2)),
            dma((max(z, 1), m)),
            dma((max(z, 1), m)),
            dma((a + z,)),
        ],
        compiler_params=pltpu.CompilerParams(collective_id=ident, has_side_effects=True),
    )(*arrays)


def scatter_kernel(n, x_ref, o_ref, one, pair, two, s1, r1, s2, r2):
    me, zed = lax.axis_index("ctx"), lax.axis_index("fsdp")
    core, chip = lax.rem(me, 2), lax.div(me, 2)
    chips = n // 2
    sib = me + 1 - 2 * core
    order = [lax.rem(chip + k, chips) for k in range(1, chips)] + [chip]
    greet([(sib, zed)] + [(2 * j + core, zed) for j in order[:-1]])
    first = []
    for k, j in enumerate(order):
        first.append(push(x_ref.at[2 * j + 1 - core], one.at[k], s1.at[k], r1.at[k], (sib, zed)))
        first[-1].start()
    second = []
    for k, j in enumerate(order):
        first[k].wait_recv()
        total = x_ref[2 * j + core].astype(F32) + one[k].astype(F32)
        if k < chips - 1:
            pair[k] = total.astype(BF)
            second.append(
                push(pair.at[k], two.at[k], s2.at[k], r2.at[k], (2 * j + core, zed))
            )
            second[-1].start()
        else:
            o_ref[...] = total
    for k in range(chips - 1):
        second[k].wait_recv()
        o_ref[...] += two[k].astype(F32)
    for copy in first + second:
        copy.wait_send()


def scatter(n, x, ident):
    _, rows, cols = x.shape
    chips = n // 2
    dma = pltpu.SemaphoreType.DMA
    return pl.pallas_call(
        functools.partial(scatter_kernel, n),
        out_shape=jax.ShapeDtypeStruct((rows, cols), F32),
        in_specs=[pl.BlockSpec(memory_space=pltpu.VMEM)],
        out_specs=pl.BlockSpec(memory_space=pltpu.VMEM),
        scratch_shapes=[
            pltpu.VMEM((chips, rows, cols), BF),
            pltpu.VMEM((chips - 1, rows, cols), BF),
            pltpu.VMEM((chips - 1, rows, cols), BF),
            dma((chips,)),
            dma((chips,)),
            dma((chips - 1,)),
            dma((chips - 1,)),
        ],
        compiler_params=pltpu.CompilerParams(
            collective_id=ident, has_side_effects=True, vmem_limit_bytes=48 << 20
        ),
    )(x)


def finish_kernel(n, m, count, *refs):
    ins, outs, lands = refs[:count], refs[count : 2 * count], refs[2 * count : 3 * count]
    z_send, z_recv, a_send, a_recv, a_fwd = refs[3 * count :]
    me, zed = lax.axis_index("ctx"), lax.axis_index("fsdp")
    core, chip = lax.rem(me, 2), lax.div(me, 2)
    chips = n // 2
    sib = me + 1 - 2 * core
    peers = [2 * lax.rem(chip + k, chips) + core for k in range(1, chips)]
    sources = [2 * lax.rem(chip + chips - k, chips) + core for k in range(1, chips)]
    zeds = [lax.rem(zed + k, m) for k in range(1, m)]
    greet([(me, z) for z in zeds] + [(sib, zed)] + [(p, zed) for p in peers])
    sums = []
    for a in range(count):
        for k, z in enumerate(zeds):
            sums.append(
                push(ins[a].at[z], lands[a].at[k], z_send.at[a, k], z_recv.at[a, k], (me, z))
            )
            sums[-1].start()
    sends = []
    for a in range(count):
        total = ins[a][zed].astype(F32)
        for k in range(m - 1):
            sums[a * (m - 1) + k].wait_recv()
            total = total + lands[a][k].astype(F32)
        outs[a][me] = total.astype(outs[a].dtype)
        own = outs[a].at[me]
        for k, p in enumerate(peers + [sib]):
            sends.append(push(own, own, a_send.at[a, k], a_recv.at[a, me], (p, zed)))
            sends[-1].start()
    for a in range(count):
        for k, s in enumerate(sources):
            slot = outs[a].at[s]
            hop = push(slot, slot, a_fwd.at[a, k], a_recv.at[a, s], (sib, zed))
            hop.wait_recv()
            hop.start()
            sends.append(hop)
    for a in range(count):
        for s in [sib] + [s + 1 - 2 * core for s in sources]:
            slot = outs[a].at[s]
            push(slot, slot, a_send.at[a, 0], a_recv.at[a, s], (sib, zed)).wait_recv()
    for copy in sums + sends:
        copy.wait_send()


def finish(n, m, arrays, ident):
    count = len(arrays)
    dma = pltpu.SemaphoreType.DMA
    vmem = pl.BlockSpec(memory_space=pltpu.VMEM)
    return pl.pallas_call(
        functools.partial(finish_kernel, n, m, count),
        out_shape=[jax.ShapeDtypeStruct((n,) + v.shape[1:], v.dtype) for v in arrays],
        in_specs=[vmem] * count,
        out_specs=[vmem] * count,
        scratch_shapes=[pltpu.VMEM((m - 1,) + v.shape[1:], v.dtype) for v in arrays]
        + [dma((count, m)), dma((count, m)), dma((count, n)), dma((count, n)), dma((count, n))],
        compiler_params=pltpu.CompilerParams(
            collective_id=ident, has_side_effects=True, vmem_limit_bytes=48 << 20
        ),
    )(*arrays)


def swap_kernel(n, x_ref, o_ref, send, recv, local):
    me, zed = lax.axis_index("ctx"), lax.axis_index("fsdp")
    others = [lax.rem(me + k, n) for k in range(1, n)]
    greet([(j, zed) for j in others])
    sends = []
    for k, j in enumerate(others):
        sends.append(push(x_ref.at[j], o_ref.at[me], send.at[k], recv.at[me], (j, zed)))
        sends[-1].start()
    own = pltpu.make_async_copy(x_ref.at[me], o_ref.at[me], local)
    own.start()
    own.wait()
    for k, j in enumerate(others):
        push(x_ref.at[j], o_ref.at[j], send.at[k], recv.at[j], (j, zed)).wait_recv()
    for copy in sends:
        copy.wait_send()


def swap(n, x, ident):
    dma = pltpu.SemaphoreType.DMA
    return pl.pallas_call(
        functools.partial(swap_kernel, n),
        out_shape=jax.ShapeDtypeStruct(x.shape, x.dtype),
        in_specs=[pl.BlockSpec(memory_space=pltpu.VMEM)],
        out_specs=pl.BlockSpec(memory_space=pltpu.VMEM),
        scratch_shapes=[dma((n,)), dma((n,)), dma],
        compiler_params=pltpu.CompilerParams(collective_id=ident, has_side_effects=True),
    )(x)


def shards(
    n,
    m,
    layer_input,
    qkv_weight,
    query_bias,
    value_bias,
    out_weight,
    out_bias,
    first_gain,
    first_shift,
    second_gain,
    second_shift,
    up_weight,
    up_bias,
    down_weight,
    down_bias,
    out_grad,
):
    seqs, block, width = layer_input.shape
    rows = seqs * block
    length = n * block
    heads = width // HD
    scale = 1.0 / math.sqrt(HD)
    me, zed = lax.axis_index("ctx"), lax.axis_index("fsdp")
    hp = -(-heads // n)
    while heads % hp:
        hp += 1
    active_n = heads // hp
    hw = hp * HD
    valid = me < active_n
    head_at = jnp.minimum(me, active_n - 1)
    share = width // m
    hidden_share = up_bias.shape[0]
    fpart = hidden_share // n
    ff = hidden_share * m
    fown = m * fpart

    x_local = layer_input.reshape(rows, width)
    g_local = out_grad.reshape(rows, width)
    qkv_own = lax.dynamic_index_in_dim(
        qkv_weight.reshape(share, 3, active_n, hw), head_at, 2, keepdims=False
    ).reshape(share, 3 * hw)
    up_own = lax.dynamic_index_in_dim(
        up_weight.reshape(share, m, n, fpart), me, 2, keepdims=False
    ).reshape(share, fown)
    down_own = lax.dynamic_index_in_dim(
        down_weight.reshape(n, fpart, width), me, 0, keepdims=False
    )
    out_cols = width // n
    out_own = lax.dynamic_slice_in_dim(out_weight, me * out_cols, out_cols, 1)
    vectors = jnp.concatenate(
        [query_bias, value_bias, out_bias, first_gain, first_shift, second_gain, second_shift,
         down_bias, up_bias]
    ).astype(F32)
    span = vectors.shape[0]
    padded = -(-span // 1024) * 1024
    vectors = jnp.pad(vectors, (0, padded - span)).reshape(padded // 128, 128)

    x_all, qkv_all, vec_all, out_all = gather(n, m, [x_local], [qkv_own, vectors, out_own], 0)
    both = jnp.stack([up_own, down_own.reshape(share, fown)])
    both = lax.all_gather(both, "fsdp", axis=1)
    up_mat = both[0].reshape(width, fown)
    down_mat = both[1].reshape(fown, width)
    out_mat = (
        lax.all_gather(out_all.reshape(width, out_cols), "ctx", axis=0)
        .transpose(1, 0, 2)
        .reshape(width, width)
    )
    g_all = lax.all_gather(g_local, "ctx", axis=0, tiled=True)

    qkv_mat = jnp.where(valid, qkv_all.reshape(width, 3 * hw), jnp.zeros((), BF))
    vec_all = vec_all.reshape(m, padded)
    pieces = [vec_all[:, i * share : (i + 1) * share].reshape(width) for i in range(8)]
    q_bias, v_bias, out_shift, gain_one, shift_one, gain_two, shift_two, down_shift = pieces
    up_shift = lax.dynamic_index_in_dim(
        vec_all[:, 8 * share : span].reshape(m, n, fpart), me, 1, keepdims=False
    ).reshape(fown)
    q_own = lax.dynamic_index_in_dim(q_bias.reshape(active_n, hw), head_at, 0, keepdims=False)
    v_own = lax.dynamic_index_in_dim(v_bias.reshape(active_n, hw), head_at, 0, keepdims=False)

    def to_seq(v):
        return (
            v.reshape(n, seqs, block, hp, HD)
            .transpose(1, 3, 0, 2, 4)
            .reshape(seqs, hp, length, HD)
        )

    def from_seq(v):
        return (
            v.reshape(seqs, hp, n, block, HD)
            .transpose(2, 0, 3, 1, 4)
            .reshape(n * rows, hw)
        )

    x_rows = x_all.reshape(n * rows, width).astype(F32)
    normed_all, _, _ = norm_rows(x_rows, gain_one, shift_one)
    mixed_in = normed_all.astype(BF)
    projected = matmul(mixed_in, qkv_mat)
    queries = to_seq((projected[:, :hw] + q_own).astype(BF))
    keys = to_seq(projected[:, hw : 2 * hw].astype(BF))
    values = to_seq((projected[:, 2 * hw :] + v_own).astype(BF))

    at = jnp.arange(length, dtype=jnp.int32)
    causal = (at[None, :] <= at[:, None])[None, None]
    scores = jnp.einsum("shqd,shkd->shqk", queries, keys, preferred_element_type=F32) * scale
    masked = jnp.where(causal, scores, NEG)
    top = jnp.max(masked, axis=-1)
    total = jnp.sum(jnp.exp(masked - top[..., None]), axis=-1)
    logsum = top + jnp.log(total)
    probs = jnp.where(causal, jnp.exp(scores - logsum[..., None]), 0.0)
    probs_b = probs.astype(BF)
    mixed = jnp.einsum("shqk,shkd->shqd", probs_b, values, preferred_element_type=F32).astype(BF)

    got = swap(n, from_seq(mixed).reshape(n, rows, hw), 1)
    attended = got[:active_n].transpose(1, 0, 2).reshape(rows, width)
    inputs = x_local.astype(F32)
    _, unit_one, inv_one = norm_rows(inputs, gain_one, shift_one)
    hidden = inputs + matmul(attended, out_mat) + out_shift
    normed_two, unit_two, inv_two = norm_rows(hidden, gain_two, shift_two)
    (ffn_in,) = gather(n, m, [normed_two.astype(BF)], [], 2)
    ffn_in = ffn_in.reshape(n * rows, width)
    lifted = matmul(ffn_in, up_mat) + up_shift
    gelu_val, gelu_slope = gelu_pair(lifted)
    active = gelu_val.astype(BF)

    grad_lifted = outer_cols(g_all, down_mat) * gelu_slope
    lifted_b = grad_lifted.astype(BF)
    part_two = outer_cols(lifted_b, up_mat).astype(BF).reshape(n, rows, width)
    grad_normed_two = scatter(n, part_two, 3)

    down_part = matmul(active, down_mat).astype(BF)
    result = hidden + down_shift + lax.psum_scatter(
        down_part, "ctx", scatter_dimension=0, tiled=True
    ).astype(F32)
    layer_output = result.astype(BF).reshape(seqs, block, width)
    grad_up_shift = jnp.sum(grad_lifted, axis=0)
    grad_down = inner_rows(active, g_all).astype(BF)
    grad_up = inner_rows(ffn_in, lifted_b).astype(BF)
    grad_down = lax.psum_scatter(grad_down, "fsdp", scatter_dimension=0, tiled=True)
    grad_up = lax.psum_scatter(grad_up, "fsdp", scatter_dimension=0, tiled=True)
    grad_down = lax.all_gather(grad_down, "ctx", axis=0, tiled=True).astype(F32)
    grad_up = (
        lax.all_gather(grad_up, "ctx", axis=0)
        .reshape(n, share, m, fpart)
        .transpose(1, 2, 0, 3)
        .reshape(share, ff)
        .astype(F32)
    )

    upstream_f = g_local.astype(F32)
    grad_gain_two = jnp.sum(grad_normed_two * unit_two, axis=0)
    grad_shift_two = jnp.sum(grad_normed_two, axis=0)
    grad_hidden = upstream_f + norm_back(grad_normed_two, unit_two, inv_two, gain_two)
    hidden_b = grad_hidden.astype(BF)
    grad_out_shift = jnp.sum(grad_hidden, axis=0)
    grad_attended = outer_cols(hidden_b, out_mat).astype(BF)
    blocks = grad_attended.reshape(rows, active_n, hw).transpose(1, 0, 2)
    blocks = jnp.pad(blocks, ((0, n - active_n), (0, 0), (0, 0)))
    grad_heads = to_seq(swap(n, blocks, 4).reshape(n * rows, hw))

    grad_out = inner_rows(attended, hidden_b).astype(BF).reshape(width, n, out_cols)
    grad_out = grad_out.transpose(1, 0, 2).reshape(n, out_cols, width)

    delta = jnp.sum(grad_heads.astype(F32) * mixed.astype(F32), axis=-1)
    grad_probs = jnp.einsum("shqd,shkd->shqk", grad_heads, values, preferred_element_type=F32)
    grad_scores = (probs * (grad_probs - delta[..., None])).astype(BF)
    grad_values = jnp.einsum("shqk,shqd->shkd", probs_b, grad_heads, preferred_element_type=F32)
    grad_queries = (
        jnp.einsum("shqk,shkd->shqd", grad_scores, keys, preferred_element_type=F32) * scale
    )
    grad_keys = (
        jnp.einsum("shqk,shqd->shkd", grad_scores, queries, preferred_element_type=F32) * scale
    )
    grad_query_shift = jnp.sum(grad_queries, axis=(0, 2)).reshape(hw)
    grad_value_shift = jnp.sum(grad_values, axis=(0, 2)).reshape(hw)
    proj_b = jnp.concatenate(
        [from_seq(g.astype(BF)) for g in (grad_queries, grad_keys, grad_values)], axis=1
    )
    part_one = outer_cols(proj_b, qkv_mat).astype(BF).reshape(n, rows, width)
    grad_qkv = inner_rows(mixed_in, proj_b).astype(BF)
    summed = scatter(n, jnp.concatenate([part_one, grad_out], axis=1), 5)
    grad_normed_one = summed[:rows]
    grad_out = summed[rows:].astype(BF).reshape(m, share, out_cols)
    grad_gain_one = jnp.sum(grad_normed_one * unit_one, axis=0)
    grad_shift_one = jnp.sum(grad_normed_one, axis=0)
    input_grad = (grad_hidden + norm_back(grad_normed_one, unit_one, inv_one, gain_one)).reshape(
        seqs, block, width
    )

    def place_heads(v):
        spot = (jnp.arange(active_n, dtype=jnp.int32) == me)[:, None]
        return jnp.where(spot, v[None, :], 0.0).reshape(width)

    spot = (jnp.arange(n, dtype=jnp.int32) == me)[None, :, None]
    up_placed = jnp.where(spot, grad_up_shift.reshape(m, 1, fpart), 0.0).reshape(ff)
    small = jnp.stack(
        [
            place_heads(grad_query_shift), place_heads(grad_value_shift), grad_out_shift,
            grad_gain_one, grad_shift_one, grad_gain_two, grad_shift_two,
            jnp.sum(upstream_f, axis=0),
        ]
    )
    small = small.reshape(8, m, share).transpose(1, 0, 2).reshape(m, 8 * share)
    small = jnp.concatenate([small, up_placed.reshape(m, hidden_share)], axis=1)
    small = jnp.pad(small, ((0, 0), (0, padded - span))).reshape(m, padded // 128, 128)
    small, grad_out, grad_qkv = finish(
        n, m, [small, grad_out, grad_qkv.reshape(m, share, 3 * hw)], 6
    )
    small = jnp.sum(small, axis=0).reshape(padded)
    mine = [small[i * share : (i + 1) * share] for i in range(8)]
    up_mine = small[8 * share : span]
    grad_out = grad_out.transpose(1, 0, 2).reshape(share, width).astype(F32)
    grad_qkv = (
        grad_qkv[:active_n]
        .reshape(active_n, share, 3, hw)
        .transpose(1, 2, 0, 3)
        .reshape(share, 3 * width)
        .astype(F32)
    )
    return (
        layer_output,
        input_grad,
        grad_qkv,
        mine[0],
        mine[1],
        grad_out,
        mine[2],
        mine[3],
        mine[4],
        mine[5],
        mine[6],
        grad_up,
        up_mine,
        grad_down,
        mine[7],
    )


def solution(mesh):
    vec, mat, act = P("fsdp"), P("fsdp", None), P("fsdp", "ctx", None)
    n, m = mesh.shape["ctx"], mesh.shape["fsdp"]
    return jax.shard_map(
        functools.partial(shards, n, m),
        mesh=mesh,
        in_specs=(act, mat, vec, vec, mat, vec, vec, vec, vec, vec, mat, vec, mat, vec, act),
        out_specs=(act, act, mat, vec, vec, mat, vec, vec, vec, vec, vec, mat, vec, mat, vec),
        check_vma=False,
    )
```

```python
import functools
import math

import jax
import jax.numpy as jnp
from jax import lax
from jax.experimental import pallas as pl
from jax.experimental.pallas import tpu as pltpu
from jax.sharding import PartitionSpec as P

HD = 64
EPS = 1e-05
NEG = -1e30
GELU_C = 0.7978845608028654
GELU_A = 0.044715
MESH = pl.DeviceIdType.MESH
BF = jnp.bfloat16
F32 = jnp.float32


def gelu_pair(values):
    inner = GELU_C * (values + GELU_A * values * values * values)
    tanh_val = jnp.tanh(inner)
    result = 0.5 * values * (1.0 + tanh_val)
    slope = 0.5 * (1.0 + tanh_val) + 0.5 * values * (1.0 - tanh_val * tanh_val) * GELU_C * (
        1.0 + 3.0 * GELU_A * values * values
    )
    return (result, slope)


def norm_rows(values, gain, shift):
    mean = jnp.mean(values, axis=-1, keepdims=True)
    centred = values - mean
    inv_std = lax.rsqrt(jnp.mean(centred * centred, axis=-1, keepdims=True) + EPS)
    normed = centred * inv_std
    return (normed * gain + shift, normed, inv_std)


def norm_back(grad_out, normed, inv_std, gain):
    scaled = grad_out * gain
    return inv_std * (
        scaled
        - jnp.mean(scaled, axis=-1, keepdims=True)
        - normed * jnp.mean(scaled * normed, axis=-1, keepdims=True)
    )


def matmul(left, right):
    return jnp.dot(left, right, preferred_element_type=F32)


def inner_rows(left, right):
    return lax.dot_general(left, right, (((0,), (0,)), ((), ())), preferred_element_type=F32)


def outer_cols(left, right):
    return lax.dot_general(left, right, (((1,), (1,)), ((), ())), preferred_element_type=F32)


def greet(devices):
    barrier = pltpu.get_barrier_semaphore()
    for device in devices:
        pl.semaphore_signal(barrier, inc=1, device_id=device, device_id_type=MESH)
    pl.semaphore_wait(barrier, len(devices))


def push(src, dst, send_sem, recv_sem, device):
    return pltpu.make_async_remote_copy(
        src_ref=src, dst_ref=dst, send_sem=send_sem, recv_sem=recv_sem,
        device_id=device, device_id_type=MESH,
    )


def gather_kernel(n, m, a_count, z_count, *refs):
    ins = refs[: a_count + z_count]
    outs = refs[a_count + z_count : 2 * (a_count + z_count)]
    a_send, a_recv, a_fwd, z_send, z_recv, local = refs[2 * (a_count + z_count) :]
    me, zed = lax.axis_index("ctx"), lax.axis_index("fsdp")
    core, chip = lax.rem(me, 2), lax.div(me, 2)
    chips = n // 2
    sib = me + 1 - 2 * core
    peers = [2 * lax.rem(chip + k, chips) + core for k in range(1, chips)]
    sources = [2 * lax.rem(chip + chips - k, chips) + core for k in range(1, chips)]
    zeds = [lax.rem(zed + k, m) for k in range(1, m)]
    devices = []
    if a_count:
        devices += [(sib, zed)] + [(p, zed) for p in peers]
    if z_count:
        devices += [(me, z) for z in zeds]
    greet(devices)
    sends = []
    locals_ = []
    for a in range(a_count):
        for k, p in enumerate(peers):
            sends.append(push(ins[a], outs[a].at[me], a_send.at[a, k], a_recv.at[a, me], (p, zed)))
            sends[-1].start()
        sends.append(
            push(ins[a], outs[a].at[me], a_send.at[a, chips - 1], a_recv.at[a, me], (sib, zed))
        )
        sends[-1].start()
    for i in range(z_count):
        b = a_count + i
        for k, z in enumerate(zeds):
            sends.append(push(ins[b], outs[b].at[zed], z_send.at[i, k], z_recv.at[i, zed], (me, z)))
            sends[-1].start()
    for b in range(a_count + z_count):
        slot = me if b < a_count else zed
        locals_.append(pltpu.make_async_copy(ins[b], outs[b].at[slot], local.at[b]))
        locals_[-1].start()
    for a in range(a_count):
        for k, s in enumerate(sources):
            push(ins[a], outs[a].at[s], a_fwd.at[a, k], a_recv.at[a, s], (sib, zed)).wait_recv()
            sends.append(
                push(outs[a].at[s], outs[a].at[s], a_fwd.at[a, k], a_recv.at[a, s], (sib, zed))
            )
            sends[-1].start()
    for a in range(a_count):
        for s in [sib] + [s + 1 - 2 * core for s in sources]:
            push(ins[a], outs[a].at[s], a_send.at[a, 0], a_recv.at[a, s], (sib, zed)).wait_recv()
    for i in range(z_count):
        b = a_count + i
        for z in zeds:
            push(ins[b], outs[b].at[z], z_send.at[i, 0], z_recv.at[i, z], (me, z)).wait_recv()
    for copy in locals_:
        copy.wait()
    for copy in sends:
        copy.wait_send()


def gather(n, m, over_ctx, over_fsdp, ident):
    arrays = tuple(over_ctx) + tuple(over_fsdp)
    a, z = len(over_ctx), len(over_fsdp)
    out_shape = [jax.ShapeDtypeStruct((n,) + v.shape, v.dtype) for v in over_ctx]
    out_shape += [jax.ShapeDtypeStruct((m,) + v.shape, v.dtype) for v in over_fsdp]
    dma = pltpu.SemaphoreType.DMA
    return pl.pallas_call(
        functools.partial(gather_kernel, n, m, a, z),
        out_shape=out_shape,
        in_specs=[pl.BlockSpec(memory_space=pl.ANY)] * (a + z),
        out_specs=[pl.BlockSpec(memory_space=pl.ANY)] * (a + z),
        scratch_shapes=[
            dma((max(a, 1), n // 2)),
            dma((max(a, 1), n)),
            dma((max(a, 1), n // 2)),
            dma((max(z, 1), m)),
            dma((max(z, 1), m)),
            dma((a + z,)),
        ],
        compiler_params=pltpu.CompilerParams(collective_id=ident, has_side_effects=True),
    )(*arrays)


def scatter_kernel(n, x_ref, o_ref, one, pair, two, s1, r1, s2, r2):
    me, zed = lax.axis_index("ctx"), lax.axis_index("fsdp")
    core, chip = lax.rem(me, 2), lax.div(me, 2)
    chips = n // 2
    sib = me + 1 - 2 * core
    order = [lax.rem(chip + k, chips) for k in range(1, chips)] + [chip]
    greet([(sib, zed)] + [(2 * j + core, zed) for j in order[:-1]])
    first = []
    for k, j in enumerate(order):
        first.append(push(x_ref.at[2 * j + 1 - core], one.at[k], s1.at[k], r1.at[k], (sib, zed)))
        first[-1].start()
    second = []
    for k, j in enumerate(order):
        first[k].wait_recv()
        total = x_ref[2 * j + core].astype(F32) + one[k].astype(F32)
        if k < chips - 1:
            pair[k] = total.astype(BF)
            second.append(
                push(pair.at[k], two.at[k], s2.at[k], r2.at[k], (2 * j + core, zed))
            )
            second[-1].start()
        else:
            o_ref[...] = total
    for k in range(chips - 1):
        second[k].wait_recv()
        o_ref[...] += two[k].astype(F32)
    for copy in first + second:
        copy.wait_send()


def scatter(n, x, ident):
    _, rows, cols = x.shape
    chips = n // 2
    dma = pltpu.SemaphoreType.DMA
    return pl.pallas_call(
        functools.partial(scatter_kernel, n),
        out_shape=jax.ShapeDtypeStruct((rows, cols), F32),
        in_specs=[pl.BlockSpec(memory_space=pltpu.VMEM)],
        out_specs=pl.BlockSpec(memory_space=pltpu.VMEM),
        scratch_shapes=[
            pltpu.VMEM((chips, rows, cols), BF),
            pltpu.VMEM((chips - 1, rows, cols), BF),
            pltpu.VMEM((chips - 1, rows, cols), BF),
            dma((chips,)),
            dma((chips,)),
            dma((chips - 1,)),
            dma((chips - 1,)),
        ],
        compiler_params=pltpu.CompilerParams(
            collective_id=ident, has_side_effects=True, vmem_limit_bytes=48 << 20
        ),
    )(x)


def finish_kernel(n, m, count, *refs):
    ins, outs, lands = refs[:count], refs[count : 2 * count], refs[2 * count : 3 * count]
    z_send, z_recv, a_send, a_recv, a_fwd = refs[3 * count :]
    me, zed = lax.axis_index("ctx"), lax.axis_index("fsdp")
    core, chip = lax.rem(me, 2), lax.div(me, 2)
    chips = n // 2
    sib = me + 1 - 2 * core
    peers = [2 * lax.rem(chip + k, chips) + core for k in range(1, chips)]
    sources = [2 * lax.rem(chip + chips - k, chips) + core for k in range(1, chips)]
    zeds = [lax.rem(zed + k, m) for k in range(1, m)]
    greet([(me, z) for z in zeds] + [(sib, zed)] + [(p, zed) for p in peers])
    sums = []
    for a in range(count):
        for k, z in enumerate(zeds):
            sums.append(
                push(ins[a].at[z], lands[a].at[k], z_send.at[a, k], z_recv.at[a, k], (me, z))
            )
            sums[-1].start()
    sends = []
    for a in range(count):
        total = ins[a][zed].astype(F32)
        for k in range(m - 1):
            sums[a * (m - 1) + k].wait_recv()
            total = total + lands[a][k].astype(F32)
        outs[a][me] = total.astype(outs[a].dtype)
        own = outs[a].at[me]
        for k, p in enumerate(peers + [sib]):
            sends.append(push(own, own, a_send.at[a, k], a_recv.at[a, me], (p, zed)))
            sends[-1].start()
    for a in range(count):
        for k, s in enumerate(sources):
            slot = outs[a].at[s]
            hop = push(slot, slot, a_fwd.at[a, k], a_recv.at[a, s], (sib, zed))
            hop.wait_recv()
            hop.start()
            sends.append(hop)
    for a in range(count):
        for s in [sib] + [s + 1 - 2 * core for s in sources]:
            slot = outs[a].at[s]
            push(slot, slot, a_send.at[a, 0], a_recv.at[a, s], (sib, zed)).wait_recv()
    for copy in sums + sends:
        copy.wait_send()


def finish(n, m, arrays, ident):
    count = len(arrays)
    dma = pltpu.SemaphoreType.DMA
    vmem = pl.BlockSpec(memory_space=pltpu.VMEM)
    return pl.pallas_call(
        functools.partial(finish_kernel, n, m, count),
        out_shape=[jax.ShapeDtypeStruct((n,) + v.shape[1:], v.dtype) for v in arrays],
        in_specs=[vmem] * count,
        out_specs=[vmem] * count,
        scratch_shapes=[pltpu.VMEM((m - 1,) + v.shape[1:], v.dtype) for v in arrays]
        + [dma((count, m)), dma((count, m)), dma((count, n)), dma((count, n)), dma((count, n))],
        compiler_params=pltpu.CompilerParams(
            collective_id=ident, has_side_effects=True, vmem_limit_bytes=48 << 20
        ),
    )(*arrays)


def swap_kernel(n, x_ref, o_ref, send, recv, local):
    me, zed = lax.axis_index("ctx"), lax.axis_index("fsdp")
    others = [lax.rem(me + k, n) for k in range(1, n)]
    greet([(j, zed) for j in others])
    sends = []
    for k, j in enumerate(others):
        sends.append(push(x_ref.at[j], o_ref.at[me], send.at[k], recv.at[me], (j, zed)))
        sends[-1].start()
    own = pltpu.make_async_copy(x_ref.at[me], o_ref.at[me], local)
    own.start()
    own.wait()
    for k, j in enumerate(others):
        push(x_ref.at[j], o_ref.at[j], send.at[k], recv.at[j], (j, zed)).wait_recv()
    for copy in sends:
        copy.wait_send()


def swap(n, x, ident):
    dma = pltpu.SemaphoreType.DMA
    return pl.pallas_call(
        functools.partial(swap_kernel, n),
        out_shape=jax.ShapeDtypeStruct(x.shape, x.dtype),
        in_specs=[pl.BlockSpec(memory_space=pltpu.VMEM)],
        out_specs=pl.BlockSpec(memory_space=pltpu.VMEM),
        scratch_shapes=[dma((n,)), dma((n,)), dma],
        compiler_params=pltpu.CompilerParams(collective_id=ident, has_side_effects=True),
    )(x)


def shards(
    n,
    m,
    layer_input,
    qkv_weight,
    query_bias,
    value_bias,
    out_weight,
    out_bias,
    first_gain,
    first_shift,
    second_gain,
    second_shift,
    up_weight,
    up_bias,
    down_weight,
    down_bias,
    out_grad,
):
    seqs, block, width = layer_input.shape
    rows = seqs * block
    length = n * block
    heads = width // HD
    scale = 1.0 / math.sqrt(HD)
    me, zed = lax.axis_index("ctx"), lax.axis_index("fsdp")
    hp = -(-heads // n)
    while heads % hp:
        hp += 1
    active_n = heads // hp
    hw = hp * HD
    valid = me < active_n
    head_at = jnp.minimum(me, active_n - 1)
    share = width // m
    hidden_share = up_bias.shape[0]
    fpart = hidden_share // n
    ff = hidden_share * m
    fown = m * fpart

    x_local = layer_input.reshape(rows, width)
    g_local = out_grad.reshape(rows, width)
    qkv_own = lax.dynamic_index_in_dim(
        qkv_weight.reshape(share, 3, active_n, hw), head_at, 2, keepdims=False
    ).reshape(share, 3 * hw)
    up_own = lax.dynamic_index_in_dim(
        up_weight.reshape(share, m, n, fpart), me, 2, keepdims=False
    ).reshape(share, fown)
    down_own = lax.dynamic_index_in_dim(
        down_weight.reshape(n, fpart, width), me, 0, keepdims=False
    )
    out_cols = width // n
    out_own = lax.dynamic_slice_in_dim(out_weight, me * out_cols, out_cols, 1)
    vectors = jnp.concatenate(
        [query_bias, value_bias, out_bias, first_gain, first_shift, second_gain, second_shift,
         down_bias, up_bias]
    ).astype(F32)
    span = vectors.shape[0]
    padded = -(-span // 1024) * 1024
    vectors = jnp.pad(vectors, (0, padded - span)).reshape(padded // 128, 128)

    x_all, g_all, qkv_all, vec_all, out_all = gather(
        n, m, [x_local, g_local], [qkv_own, vectors, out_own], 0
    )
    g_all = g_all.reshape(n * rows, width)
    out_mat = (
        lax.all_gather(out_all.reshape(width, out_cols), "ctx", axis=0)
        .transpose(1, 0, 2)
        .reshape(width, width)
    )

    qkv_mat = jnp.where(valid, qkv_all.reshape(width, 3 * hw), jnp.zeros((), BF))
    vec_all = vec_all.reshape(m, padded)
    pieces = [vec_all[:, i * share : (i + 1) * share].reshape(width) for i in range(8)]
    q_bias, v_bias, out_shift, gain_one, shift_one, gain_two, shift_two, down_shift = pieces
    up_shift = lax.dynamic_index_in_dim(
        vec_all[:, 8 * share : span].reshape(m, n, fpart), me, 1, keepdims=False
    ).reshape(fown)
    q_own = lax.dynamic_index_in_dim(q_bias.reshape(active_n, hw), head_at, 0, keepdims=False)
    v_own = lax.dynamic_index_in_dim(v_bias.reshape(active_n, hw), head_at, 0, keepdims=False)

    def to_seq(v):
        return (
            v.reshape(n, seqs, block, hp, HD)
            .transpose(1, 3, 0, 2, 4)
            .reshape(seqs, hp, length, HD)
        )

    def from_seq(v):
        return (
            v.reshape(seqs, hp, n, block, HD)
            .transpose(2, 0, 3, 1, 4)
            .reshape(n * rows, hw)
        )

    x_rows = x_all.reshape(n * rows, width).astype(F32)
    normed_all, _, _ = norm_rows(x_rows, gain_one, shift_one)
    mixed_in = normed_all.astype(BF)
    both = jnp.stack([up_own, down_own.reshape(share, fown)])
    both, mixed_in = lax.optimization_barrier((both, mixed_in))
    both = lax.all_gather(both, "fsdp", axis=1)
    up_mat = both[0].reshape(width, fown)
    down_mat = both[1].reshape(fown, width)
    projected = matmul(mixed_in, qkv_mat)
    queries = to_seq((projected[:, :hw] + q_own).astype(BF))
    keys = to_seq(projected[:, hw : 2 * hw].astype(BF))
    values = to_seq((projected[:, 2 * hw :] + v_own).astype(BF))

    at = jnp.arange(length, dtype=jnp.int32)
    causal = (at[None, :] <= at[:, None])[None, None]
    scores = jnp.einsum("shqd,shkd->shqk", queries, keys, preferred_element_type=F32) * scale
    masked = jnp.where(causal, scores, NEG)
    top = jnp.max(masked, axis=-1)
    total = jnp.sum(jnp.exp(masked - top[..., None]), axis=-1)
    logsum = top + jnp.log(total)
    probs = jnp.where(causal, jnp.exp(scores - logsum[..., None]), 0.0)
    probs_b = probs.astype(BF)
    mixed = jnp.einsum("shqk,shkd->shqd", probs_b, values, preferred_element_type=F32).astype(BF)

    got = swap(n, from_seq(mixed).reshape(n, rows, hw), 1)
    attended = got[:active_n].transpose(1, 0, 2).reshape(rows, width)
    inputs = x_local.astype(F32)
    _, unit_one, inv_one = norm_rows(inputs, gain_one, shift_one)
    hidden = inputs + matmul(attended, out_mat) + out_shift
    normed_two, unit_two, inv_two = norm_rows(hidden, gain_two, shift_two)
    (ffn_in,) = gather(n, m, [normed_two.astype(BF)], [], 2)
    ffn_in = ffn_in.reshape(n * rows, width)
    lifted = matmul(ffn_in, up_mat) + up_shift
    gelu_val, gelu_slope = gelu_pair(lifted)
    active = gelu_val.astype(BF)

    grad_lifted = outer_cols(g_all, down_mat) * gelu_slope
    lifted_b = grad_lifted.astype(BF)
    part_two = outer_cols(lifted_b, up_mat).astype(BF).reshape(n, rows, width)
    down_part = matmul(active, down_mat).astype(BF).reshape(n, rows, width)
    summed = scatter(n, jnp.concatenate([part_two, down_part], axis=1), 3)
    grad_normed_two = summed[:rows]

    result = hidden + down_shift + summed[rows:]
    layer_output = result.astype(BF).reshape(seqs, block, width)
    grad_up_shift = jnp.sum(grad_lifted, axis=0)
    grad_down = inner_rows(active, g_all).astype(BF)
    grad_up = inner_rows(ffn_in, lifted_b).astype(BF)
    grad_down = lax.psum_scatter(grad_down, "fsdp", scatter_dimension=0, tiled=True)
    grad_up = lax.psum_scatter(grad_up, "fsdp", scatter_dimension=0, tiled=True)
    grad_down = lax.all_gather(grad_down, "ctx", axis=0, tiled=True).astype(F32)
    grad_up = (
        lax.all_gather(grad_up, "ctx", axis=0)
        .reshape(n, share, m, fpart)
        .transpose(1, 2, 0, 3)
        .reshape(share, ff)
        .astype(F32)
    )

    upstream_f = g_local.astype(F32)
    grad_gain_two = jnp.sum(grad_normed_two * unit_two, axis=0)
    grad_shift_two = jnp.sum(grad_normed_two, axis=0)
    grad_hidden = upstream_f + norm_back(grad_normed_two, unit_two, inv_two, gain_two)
    hidden_b = grad_hidden.astype(BF)
    grad_out_shift = jnp.sum(grad_hidden, axis=0)
    grad_attended = outer_cols(hidden_b, out_mat).astype(BF)
    blocks = grad_attended.reshape(rows, active_n, hw).transpose(1, 0, 2)
    blocks = jnp.pad(blocks, ((0, n - active_n), (0, 0), (0, 0)))
    grad_heads = to_seq(swap(n, blocks, 4).reshape(n * rows, hw))

    grad_out = inner_rows(attended, hidden_b).astype(BF).reshape(width, n, out_cols)
    grad_out = grad_out.transpose(1, 0, 2).reshape(n, out_cols, width)

    delta = jnp.sum(grad_heads.astype(F32) * mixed.astype(F32), axis=-1)
    grad_probs = jnp.einsum("shqd,shkd->shqk", grad_heads, values, preferred_element_type=F32)
    grad_scores = (probs * (grad_probs - delta[..., None])).astype(BF)
    grad_values = jnp.einsum("shqk,shqd->shkd", probs_b, grad_heads, preferred_element_type=F32)
    grad_queries = (
        jnp.einsum("shqk,shkd->shqd", grad_scores, keys, preferred_element_type=F32) * scale
    )
    grad_keys = (
        jnp.einsum("shqk,shqd->shkd", grad_scores, queries, preferred_element_type=F32) * scale
    )
    grad_query_shift = jnp.sum(grad_queries, axis=(0, 2)).reshape(hw)
    grad_value_shift = jnp.sum(grad_values, axis=(0, 2)).reshape(hw)
    proj_b = jnp.concatenate(
        [from_seq(g.astype(BF)) for g in (grad_queries, grad_keys, grad_values)], axis=1
    )
    part_one = outer_cols(proj_b, qkv_mat).astype(BF).reshape(n, rows, width)
    grad_qkv = inner_rows(mixed_in, proj_b).astype(BF)
    summed = scatter(n, jnp.concatenate([part_one, grad_out], axis=1), 5)
    grad_normed_one = summed[:rows]
    grad_out = summed[rows:].astype(BF).reshape(m, share, out_cols)
    grad_gain_one = jnp.sum(grad_normed_one * unit_one, axis=0)
    grad_shift_one = jnp.sum(grad_normed_one, axis=0)
    input_grad = (grad_hidden + norm_back(grad_normed_one, unit_one, inv_one, gain_one)).reshape(
        seqs, block, width
    )

    def place_heads(v):
        spot = (jnp.arange(active_n, dtype=jnp.int32) == me)[:, None]
        return jnp.where(spot, v[None, :], 0.0).reshape(width)

    spot = (jnp.arange(n, dtype=jnp.int32) == me)[None, :, None]
    up_placed = jnp.where(spot, grad_up_shift.reshape(m, 1, fpart), 0.0).reshape(ff)
    small = jnp.stack(
        [
            place_heads(grad_query_shift), place_heads(grad_value_shift), grad_out_shift,
            grad_gain_one, grad_shift_one, grad_gain_two, grad_shift_two,
            jnp.sum(upstream_f, axis=0),
        ]
    )
    small = small.reshape(8, m, share).transpose(1, 0, 2).reshape(m, 8 * share)
    small = jnp.concatenate([small, up_placed.reshape(m, hidden_share)], axis=1)
    small = jnp.pad(small, ((0, 0), (0, padded - span))).reshape(m, padded // 128, 128)
    small, grad_out, grad_qkv = finish(
        n, m, [small, grad_out, grad_qkv.reshape(m, share, 3 * hw)], 6
    )
    small = jnp.sum(small, axis=0).reshape(padded)
    mine = [small[i * share : (i + 1) * share] for i in range(8)]
    up_mine = small[8 * share : span]
    grad_out = grad_out.transpose(1, 0, 2).reshape(share, width).astype(F32)
    grad_qkv = jnp.concatenate(
        [grad_qkv[a, :, t * hw : (t + 1) * hw] for t in range(3) for a in range(active_n)], axis=1
    ).astype(F32)
    return (
        layer_output,
        input_grad,
        grad_qkv,
        mine[0],
        mine[1],
        grad_out,
        mine[2],
        mine[3],
        mine[4],
        mine[5],
        mine[6],
        grad_up,
        up_mine,
        grad_down,
        mine[7],
    )


def solution(mesh):
    vec, mat, act = P("fsdp"), P("fsdp", None), P("fsdp", "ctx", None)
    n, m = mesh.shape["ctx"], mesh.shape["fsdp"]
    return jax.shard_map(
        functools.partial(shards, n, m),
        mesh=mesh,
        in_specs=(act, mat, vec, vec, mat, vec, vec, vec, vec, vec, mat, vec, mat, vec, act),
        out_specs=(act, act, mat, vec, vec, mat, vec, vec, vec, vec, vec, mat, vec, mat, vec),
        check_vma=False,
    )
```
